256 devices in a mesh: dp: 4 (over x), ctx: 16 (over y_hi, z), tensor: 4 (over y_lo, core).
Axes of the slice: x: 4, y: 4 (y_hi: 2, y_lo: 2; y = y_hi * 2 + y_lo), z: 8, core: 2. Of those that a mesh axis runs over, the one named last changes fastest.
Arguments:
- residues: bfloat16 [8192, 2560], P(('dp', 'ctx')), parts along dimension 0, may hold values from -6 to 6
- chain_ids: int32 [8192], P(('dp', 'ctx')), parts along dimension 0, may hold values from 0 to 3, never falling along the last dimension, each value on 1 to 1024 neighbouring positions
- residue_valid: int32 [8192], P(('dp', 'ctx')), parts along dimension 0, may hold values from 0 to 1, as said below
- layer_weights: bfloat16 [4, 2560, 1536], P(None, 'ctx', 'tensor')
- resampler_weights: bfloat16 [4, 2560, 1536], P(None, 'ctx', 'tensor')
- norm_gains: float32 [3, 2560], replicated, may hold values from 0.25 to 1.75
- norm_biases: float32 [3, 2560], replicated, may hold values from -2 to 2
- latents: bfloat16 [128, 2560], replicated, may hold values from -6 to 6
Outputs:
- hidden_states: bfloat16 [8192, 2560], P(('dp', 'ctx'), 'tensor'), parts along dimension 0
- latent_out: bfloat16 [512, 2560], P(('dp', 'ctx'), 'tensor'), parts along dimension 0
The draws below stay inside these ranges and needn't reach their ends.
There are 4 independent parts, one for each index of `dp`. The reference program is written for one: setup_inputs(seed, part) draws one part's arguments, and reference() takes and returns one part's arrays. A program takes and returns all parts, laid end to end along the dimension named above; an argument that names none is the same for every part. Nothing has to cross between parts.
Inputs may be any that keep to these rules, and one draw needn't show every extreme that they name: `chain_ids`: ids never fall along the group; 4 chains of 1 to 1024 residues, one of exactly 1024. `residue_valid`: the group's first residue is always 1.
All inputs are finite; a program needn't handle non-finite values.
Results may differ from the reference program's by a relative error of at most 0.034.
The reference program's roundings to bfloat16 on the way count: a program that leaves them out, or rounds other values in their place, can miss the bound.
Values may be sent and summed in bfloat16 or wider, within the bound.
A program may use at most 64 MiB of HBM per device.

```python
import math
import jax
import jax.numpy as jnp
import numpy as np
from jax import lax

D = 2560
HEADS = 24
HDIM = 64
LATENTS = 128
CHAINS = 4
LENGTH = 2048
MOST = 1024


def stacked_weights(key, out_fan, low_strength, high_strength):
    key_query, key_key, key_value, key_out, key_align = jax.random.split(key, 5)
    mat_shape = (D, HEADS * HDIM)
    w_query = jax.random.normal(key_query, mat_shape, jnp.float32) * (2.0 / D) ** 0.5
    w_key = jax.random.normal(key_key, mat_shape, jnp.float32) * (2.0 / D) ** 0.5
    w_value = jax.random.normal(key_value, mat_shape, jnp.float32) * (1.0 / D) ** 0.5
    w_out = jax.random.normal(key_out, mat_shape, jnp.float32) * out_fan ** (-0.5)
    strength = jax.random.uniform(key_align, (HEADS, 1), jnp.float32, low_strength, high_strength)
    per_column = jnp.broadcast_to(strength, (HEADS, HDIM)).reshape(1, HEADS * HDIM)
    w_key = per_column * w_query + w_key
    return jnp.stack([w_query, w_key, w_value, w_out]).astype(jnp.bfloat16)


def draw_layer_weights(key, part):
    key = jax.random.fold_in(key, 11)
    return stacked_weights(key, 32.0, 0.0, 0.0)


def draw_resampler_weights(key, part):
    key = jax.random.fold_in(key, 12)
    return stacked_weights(key, 16.0, 0.0, 0.0)


def draw_residue_valid(key, part):
    key = jax.random.fold_in(key, 13)
    coin = jax.random.randint(key, (LENGTH,), 0, 8)
    return jnp.where(coin < 7, 1, 0).astype(jnp.int32).at[0].set(1)


def block_levels(key, shape, pieces, smallest, top_value):
    def one(dim, parts):
        heights = jax.random.uniform(jax.random.fold_in(jax.random.fold_in(key, 6), dim), (parts,), jnp.float32, smallest / len(pieces), top_value / len(pieces))
        return jnp.repeat(jnp.exp(heights), shape[dim] // parts).reshape((-1,) + (1,) * (len(shape) - dim - 1))

    gain = one(*pieces[0])
    for cut in pieces[1:]:
        gain = gain * one(*cut)
    return gain


def length_profile(count, total, most, skew):
    weights = [(1 << 20) // math.isqrt(standing ** skew) + 1 for standing in range(2, count + 1)]
    surplus, given = total - most - (count - 1), [1] * (count - 1)
    while surplus > 0:
        candidates = [i for i in range(count - 1) if given[i] < most]
        mass, remaining = sum([weights[i] for i in candidates]), surplus
        for i in candidates:
            extra = min(most - given[i], max(1, remaining * weights[i] // mass), surplus)
            given[i] = given[i] + extra
            surplus = surplus - extra
    return np.array([most] + given)


def ragged_sizes(key, count, total, bound, skew):
    if count == 2:
        one = jax.random.randint(key, (), max(1, total - bound), min(bound, total - 1) + 1)
        return jnp.stack([one, total - one])
    sizes = jnp.asarray(length_profile(count, total, bound, skew), jnp.int32)
    pairs = (count - 1) // 2
    donor, receiver = sizes[1:1 + 2 * pairs:2], sizes[2:2 + 2 * pairs:2]
    slack = jnp.minimum(donor - 1, bound - receiver)
    moved = jax.random.randint(jax.random.fold_in(key, 1), (pairs,), 0, 1 << 20) % (slack + 1)
    sizes = sizes.at[1:1 + 2 * pairs:2].set(donor - moved).at[2:2 + 2 * pairs:2].set(receiver + moved)
    return sizes[jax.random.permutation(jax.random.fold_in(key, 2), count)]


def gaussian(rng, extent, scale, most, cuts=(), held_as=jnp.bfloat16):
    array = scale * jax.random.normal(rng, extent, jnp.float32)
    if cuts:
        array = array * block_levels(rng, extent, cuts, -0.22, 0.18)
    return jnp.clip(array, -most, most).astype(held_as)


def setup_inputs(seed: int = 0, part: int = 0) -> dict:
    keys = jax.random.split(jax.random.key(seed), 9)
    part_splits = jax.random.split(jax.random.fold_in(keys[8], part), 9)
    return {
        "residues": gaussian(part_splits[0], (LENGTH, D), 1.0, 6.0, ((0, 16),)),
        "chain_ids": jnp.searchsorted(jnp.cumsum(ragged_sizes(part_splits[1], CHAINS, LENGTH, MOST, 0)), jnp.arange(LENGTH), side="right").astype(jnp.int32),
        "residue_valid": draw_residue_valid(jax.random.fold_in(jax.random.fold_in(keys[8], part), 71), part),
        "layer_weights": draw_layer_weights(jax.random.fold_in(keys[8], 71), part),
        "resampler_weights": draw_resampler_weights(jax.random.fold_in(keys[8], 71), part),
        "norm_gains": jnp.clip(1.0 + 0.15 * jax.random.normal(keys[5], (3, D), jnp.float32), 0.25, 1.75),
        "norm_biases": gaussian(keys[6], (3, D), 0.3, 2.0, (), jnp.float32),
        "latents": gaussian(keys[7], (LATENTS, D), 1.0, 6.0),
    }


NEGATIVE = -1e+30
EPSILON = 1e-05

def layer_norm(matrix, gain_row, bias_row):
    as_float = matrix.astype(jnp.float32)
    average = lax.optimization_barrier(jnp.mean(as_float, axis=-1, keepdims=True))
    centred = as_float - average
    variance = lax.optimization_barrier(jnp.mean(centred * centred, axis=-1, keepdims=True))
    return centred * lax.rsqrt(variance + EPSILON) * gain_row.astype(jnp.float32) + bias_row.astype(jnp.float32)

def rotary(matrix, positions, head_dim):
    row_count = matrix.shape[0]
    per_head = matrix.reshape(row_count, -1, head_dim)
    half_dim = head_dim // 2
    frequency = jnp.exp(jnp.arange(half_dim, dtype=jnp.float32) * (-2.0 * math.log(10000.0) / head_dim))
    angles = positions.astype(jnp.float32)[:, None] * frequency[None, :]
    cos_part = jnp.cos(angles)[:, None, :]
    sin_part = jnp.sin(angles)[:, None, :]
    lower_half = per_head[..., :half_dim]
    upper_half = per_head[..., half_dim:]
    turned = jnp.concatenate([lower_half * cos_part - upper_half * sin_part, upper_half * cos_part + lower_half * sin_part], axis=-1)
    return turned.reshape(row_count, -1)

def contract_last(left, right):
    return lax.dot_general(left, right, (((1,), (1,)), ((), ())), preferred_element_type=jnp.float32)

def split_heads(matrix):
    return matrix.reshape(matrix.shape[0], HEADS, HDIM).transpose(1, 0, 2)

def reference(residues, chain_ids, residue_valid, layer_weights, resampler_weights, norm_gains, norm_biases, latents):
    length = residues.shape[0]
    q_scale = HDIM ** (-0.5)
    positions = jnp.arange(length, dtype=jnp.int32)
    normed = layer_norm(residues, norm_gains[0], norm_biases[0]).astype(jnp.bfloat16)
    queries = rotary(jnp.dot(normed, layer_weights[0], preferred_element_type=jnp.float32) * q_scale, positions, HDIM).astype(jnp.bfloat16)
    key_rows = rotary(jnp.dot(normed, layer_weights[1], preferred_element_type=jnp.float32), positions, HDIM).astype(jnp.bfloat16)
    value_rows = jnp.dot(normed, layer_weights[2], preferred_element_type=jnp.float32).astype(jnp.bfloat16)
    key_tags = jnp.where(residue_valid > 0, chain_ids, -1).astype(jnp.int32)
    query_heads = split_heads(queries)
    key_heads = split_heads(key_rows)
    value_heads = split_heads(value_rows)
    block_rows = math.gcd(length, 512)

    def attend_block(block_index):
        offset = (block_index * block_rows).astype(jnp.int32)
        own_chain = lax.dynamic_slice_in_dim(chain_ids, offset, block_rows, 0)
        own_pos = offset + jnp.arange(block_rows, dtype=jnp.int32)
        allowed = (own_chain[:, None] == key_tags[None, :]) | (own_pos[:, None] == positions[None, :])

        def one_head(operands):
            head_query, head_key, head_value = operands
            block_query = lax.dynamic_slice_in_dim(head_query, offset, block_rows, 0)
            scores = jnp.dot(block_query, head_key.T, preferred_element_type=jnp.float32)
            scores = jnp.where(allowed, scores, NEGATIVE)
            maximum = lax.optimization_barrier(jnp.max(scores, axis=1, keepdims=True))
            unrounded = jnp.where(allowed, jnp.exp(scores - maximum), 0.0)
            totals = lax.optimization_barrier(jnp.sum(unrounded, axis=1, keepdims=True))
            mixture = jnp.dot(unrounded.astype(jnp.bfloat16), head_value, preferred_element_type=jnp.float32)
            return mixture / totals
        per_head = lax.map(one_head, (query_heads, key_heads, value_heads))
        return per_head.transpose(1, 0, 2).reshape(block_rows, HEADS * HDIM).astype(jnp.bfloat16)
    attended = lax.map(attend_block, jnp.arange(length // block_rows, dtype=jnp.int32)).reshape(length, HEADS * HDIM)
    updated = residues.astype(jnp.float32) + contract_last(attended, layer_weights[3])
    hidden_states = updated.astype(jnp.bfloat16)
    residue_normed = layer_norm(updated, norm_gains[1], norm_biases[1]).astype(jnp.bfloat16)
    latent_normed = layer_norm(latents, norm_gains[2], norm_biases[2]).astype(jnp.bfloat16)
    latent_query = (jnp.dot(latent_normed, resampler_weights[0], preferred_element_type=jnp.float32) * q_scale).astype(jnp.bfloat16)
    residue_key = jnp.dot(residue_normed, resampler_weights[1], preferred_element_type=jnp.float32).astype(jnp.bfloat16)
    residue_value = jnp.dot(residue_normed, resampler_weights[2], preferred_element_type=jnp.float32).astype(jnp.bfloat16)
    usable = residue_valid > 0

    def latent_head(operands):
        head_query, head_key, head_value = operands
        scores = jnp.dot(head_query, head_key.T, preferred_element_type=jnp.float32)
        scores = jnp.where(usable[None, :], scores, NEGATIVE)
        maximum = lax.optimization_barrier(jnp.max(scores, axis=1, keepdims=True))
        unrounded = jnp.where(usable[None, :], jnp.exp(scores - maximum), 0.0)
        totals = lax.optimization_barrier(jnp.sum(unrounded, axis=1, keepdims=True))
        mixture = jnp.dot(unrounded.astype(jnp.bfloat16), head_value, preferred_element_type=jnp.float32)
        return mixture / totals
    latent_heads = lax.map(latent_head, (split_heads(latent_query), split_heads(residue_key), split_heads(residue_value)))
    latent_attended = latent_heads.transpose(1, 0, 2).reshape(latents.shape[0], HEADS * HDIM).astype(jnp.bfloat16)
    latent_out = (latents.astype(jnp.float32) + contract_last(latent_attended, resampler_weights[3])).astype(jnp.bfloat16)
    return (hidden_states, latent_out)
```

```python
import functools
import math

import jax
import jax.numpy as jnp
import numpy as np
from jax import lax
from jax.experimental import pallas as pl
from jax.experimental.pallas import tpu as pltpu
from jax.sharding import PartitionSpec as P

HDIM = 64
NEGATIVE = -1e30
EPSILON = 1e-05
ROWS = 128
COLS = 384
WIDTH = 2560
DEPTH = 160
HALF = 80
CUT = 48
SLICE = 640
BLOCKS = 16
RING = 8
MESH = pl.DeviceIdType.MESH
F32 = jnp.float32
BF16 = jnp.bfloat16


def angle_tables():
    half = HDIM // 2
    freq = np.exp(np.arange(half, dtype=np.float32) * np.float32(-2.0 * math.log(10000.0) / HDIM))
    lanes = np.tile(np.concatenate([freq, freq]), COLS // HDIM).astype(np.float64)
    inner = np.arange(ROWS)[:, None] * lanes[None, :]
    outer = (np.arange(BLOCKS) * ROWS)[:, None] * lanes[None, :]
    return [t.astype(np.float32) for t in (np.cos(inner), np.sin(inner), np.cos(outer), np.sin(outer))]


def normalised(x, gain, bias):
    average = jnp.mean(x, axis=-1, keepdims=True)
    centred = x - average
    variance = jnp.mean(centred * centred, axis=-1, keepdims=True)
    return centred * lax.rsqrt(variance + EPSILON) * gain + bias


def contract_last(left, right):
    return lax.dot_general(left, right, (((1,), (1,)), ((), ())), preferred_element_type=F32)


def pair_stack(pair):
    lane = lax.broadcasted_iota(jnp.int32, pair.shape, 1)
    wide = pair.astype(F32)
    first = jnp.where(lane < HDIM, wide, 0.0)
    second = jnp.where(lane < HDIM, 0.0, wide)
    return jnp.concatenate([first, second], axis=0).astype(BF16)


def kernel(
    res_ref, chain_ref, valid_ref, lw_ref, rw_ref, gain_hbm, bias_hbm, lat_hbm, ci_hbm, si_hbm, co_hbm, so_hbm,
    hid_ref, out_ref,
    wb, xb, chain_row, valid_row, gain_ref, bias_ref, lat_ref, ci_ref, si_ref, co_ref, so_ref,
    kvb, att, hb, ho, rn, lq, rkv, pk, rb, lp, lb, lat32, fin,
    load_s, perm_s, perm_r, ring_s, ring_r, x_s, x_r, xx_s, xx_r, sib_s, sib_r,
    kv_s, kv_r, kvs_s, kvs_r, rs_s, rs_r, ag_s, ag_r, ho_s, ho_r, a2_s, a2_r, lo_s, lo_r,
):
    x = lax.axis_index("dp")
    ctx = lax.axis_index("ctx")
    ten = lax.axis_index("tensor")
    y_hi, z = lax.div(ctx, 8), lax.rem(ctx, 8)
    y_lo, core = lax.div(ten, 2), lax.rem(ten, 2)
    r = core * 8 + z
    group = y_lo * 2 + y_hi
    native = y_hi == core
    moved = y_hi != core

    def dev(yh, yl, zz, cc, xx=x):
        return (xx, yh * 8 + zz, yl * 2 + cc)

    def zpos(shift):
        return lax.rem(z + (shift % 8), 8)

    right = dev(y_hi, y_lo, zpos(1), core)
    left = dev(y_hi, y_lo, zpos(-1), core)
    sibling = dev(y_hi, y_lo, z, 1 - core)
    partner = dev(1 - y_hi, y_lo, z, 1 - core)
    z_hi, z_lo = lax.div(z, 4), lax.rem(z, 4)
    out_to = dev(z_hi, y_hi, core * 4 + z_lo, y_lo)
    out_from = dev(y_lo, core, y_hi * 4 + z_lo, z_hi)
    out_stays = (y_hi == y_lo) & (y_lo == core) & (core == z_hi)
    out_moves = jnp.logical_not(out_stays)
    opposite = dev(1 - y_hi, 1 - y_lo, z, core)
    x_up = dev(y_hi, y_lo, z, core, lax.rem(x + 1, 4))
    x_down = dev(y_hi, y_lo, z, core, lax.rem(x + 3, 4))

    def peer(offset):
        return lax.rem(group + offset, 4)

    def group_device(g):
        return dev(lax.rem(g, 2), lax.div(g, 2), z, core)

    barrier = pltpu.get_barrier_semaphore()
    greeted = [right, left, sibling, partner, x_up, x_down, out_from] + [group_device(peer(k)) for k in range(1, 4)]
    for device in greeted:
        pl.semaphore_signal(barrier, inc=1, device_id=device, device_id_type=MESH)
    loads = [
        pltpu.make_async_copy(src, dst, load_s.at[k])
        for k, (src, dst) in enumerate(
            [
                (gain_hbm, gain_ref), (bias_hbm, bias_ref), (lat_hbm, lat_ref), (ci_hbm, ci_ref),
                (si_hbm, si_ref), (co_hbm, co_ref), (so_hbm, so_ref),
            ]
        )
    ]
    for load in loads:
        load.start()
    pl.semaphore_wait(barrier, len(greeted))

    def remote(src, dst, ss, rr, device):
        return pltpu.make_async_remote_copy(
            src_ref=src, dst_ref=dst, send_sem=ss, recv_sem=rr, device_id=device, device_id_type=MESH
        )

    def arrived(ref, rr):
        remote(ref, ref, load_s.at[0], rr, sibling).wait_recv()

    def begin(copy):
        copy.start()

    def sent(ref, ss):
        remote(ref, ref, ss, load_s.at[0], sibling).wait_send()

    half = lax.rem(x, 2)

    def piece_z(index):
        step = (index + 1) // 2
        return zpos(-step if index % 2 else step)

    def area(mat, mats, owner, index, offset, rows):
        start = (owner * 8 + piece_z(index)) * DEPTH + offset
        return wb.at[pl.ds(mat, mats), pl.ds(pl.multiple_of(start, 16), rows), :]

    x_moves = [
        (res_ref, xb, 0), (chain_ref, chain_row, 1), (valid_ref, valid_row, 2),
    ]

    def x_copy(k):
        src, dst, sem = x_moves[k]
        return remote(src, dst, perm_s.at[sem], perm_r.at[sem], opposite)

    def x_local(k):
        src, dst, sem = x_moves[k]
        return pltpu.make_async_copy(src, dst, perm_r.at[sem])

    class Chunk:
        def __init__(self, number, source, first, second, quarter):
            self.number, self.mat, self.quarter = number, 2 * number, quarter
            self.source, self.pair = source, (first, second)
            self.x_done = self.xx_done = self.sib_done = 0

        def own(self, offset=0, rows=HALF):
            if self.quarter:
                return self.mat + lax.div(x, 2), 1, half * HALF + offset, rows
            return self.mat, 2, half * HALF + offset, rows

        def of_plane(self, plane, offset=0, rows=HALF):
            plane = lax.rem(plane, 4)
            return self.mat + lax.div(plane, 2), 1, lax.rem(plane, 2) * HALF + offset, rows

        def at(self, owner, index, what):
            mat, mats, offset, rows = what
            return area(mat, mats, owner, index, offset, rows)

        def moves(self):
            rows = pl.ds(pl.multiple_of(half * HALF, 16), HALF)
            first, second = self.pair
            sem = 3 + 2 * self.number
            if self.quarter:
                src = self.source.at[pl.ds(first + (second - first) * lax.div(x, 2), 1), rows, :]
                return [(src, self.own(), sem)]
            if second == first + 1:
                return [(self.source.at[pl.ds(first, 2), rows, :], self.own(), sem)]
            return [
                (self.source.at[pl.ds(m, 1), rows, :], (self.mat + k, 1, half * HALF, HALF), sem + k)
                for k, m in enumerate(self.pair)
                if (self.number, k) != (1, 1)
            ]

        def perm_copies(self):
            out = []
            for src, what, sem in self.moves():
                mat, mats, offset, rows = what
                start = (y_hi * 8 + z) * DEPTH + offset
                there = wb.at[pl.ds(mat, mats), pl.ds(pl.multiple_of(start, 16), rows), :]
                out.append(remote(src, there, perm_s.at[sem], perm_r.at[sem], partner))
            return out

        def perm_start(self):
            @pl.when(native)
            def _():
                for src, what, sem in self.moves():
                    pltpu.make_async_copy(src, self.at(core, 0, what), perm_r.at[sem]).start()

            @pl.when(moved)
            def _():
                for copy in self.perm_copies():
                    copy.start()

        def perm_wait(self):
            @pl.when(native)
            def _():
                for src, what, sem in self.moves():
                    pltpu.make_async_copy(src, self.at(core, 0, what), perm_r.at[sem]).wait()

            @pl.when(moved)
            def _():
                for src, what, sem in self.moves():
                    arrived(self.at(core, 0, what), perm_r.at[sem])

        def ring_copy(self, index, arriving, what, sem):
            ref = self.at(core, index, what)
            target = right if arriving % 2 else left
            return remote(ref, ref, ring_s.at[self.number], ring_r.at[self.number, sem], target)

        def last(self, way):
            if self.quarter:
                return self.own(*((0, CUT), (CUT, HALF - CUT))[way])
            return self.mat + way, 1, half * HALF, HALF

        def x_out(self, side):
            if self.quarter:
                return self.own()
            return self.mat + side, 1, half * HALF, HALF

        def xx_rows(self, side):
            return ((0, CUT), (CUT, HALF - CUT))[side]

        def spread(self, index):
            if index == 0:
                begin(self.ring_copy(0, 1, self.own(), 1))
                begin(self.ring_copy(0, 2, self.own(), 2))
            elif index <= 4:
                begin(self.ring_copy(index, index + 2, self.own(), index + 2))
            elif index <= 6:
                begin(self.ring_copy(index, index, self.last(index - 5), 7))
            if not self.quarter:
                self.sib_start(index, half * HALF, HALF)
            for side in range(2):
                ref = self.at(core, index, self.x_out(side))
                begin(remote(ref, ref, x_s.at[self.number], x_r.at[self.number, index], (x_up, x_down)[side]))

        def ring_wait(self, index):
            arrived(self.at(core, index, self.own()), ring_r.at[self.number, index])

        def x_next(self):
            index = self.x_done
            self.x_done += 1
            arrived(self.at(core, index, (self.mat, 2, 0, HALF)), x_r.at[self.number, index])
            if self.quarter:
                for side in range(2):
                    ref = self.at(core, index, self.of_plane(x + (3, 1)[side], *self.xx_rows(side)))
                    begin(remote(ref, ref, xx_s, xx_r.at[index], (x_up, x_down)[side]))
            else:
                self.sib_start(index, (1 - half) * HALF, HALF)

        def xx_next(self):
            index = self.xx_done
            self.xx_done += 1
            arrived(self.at(core, index, (self.mat, 1, 0, HALF)), xx_r.at[index])
            self.sib_start(index)

        def sib_start(self, index, offset=0, rows=DEPTH):
            ref = self.at(core, index, (self.mat, 2, offset, rows))
            begin(remote(ref, ref, sib_s.at[self.number], sib_r.at[self.number], sibling))

        def step(self, number):
            if number == 0:
                self.spread(0)
                return
            for index in (2 * number - 1, 2 * number):
                if index <= 7:
                    self.ring_wait(index)
                    self.spread(index)
            while self.x_done < 2 * number - 1:
                self.x_next()
            while self.quarter and self.xx_done < 2 * number - 3:
                self.xx_next()

        def finish(self):
            while self.x_done < 8:
                self.x_next()
            while self.quarter and self.xx_done < 8:
                self.xx_next()
            rows = pl.ds(pl.multiple_of((1 - core) * 8 * DEPTH, 16), 8 * DEPTH)
            arrived(wb.at[pl.ds(self.mat, 2), rows, :], sib_r.at[self.number])

        def all_sent(self):
            mats = 1 if self.quarter else 2
            sent(wb.at[pl.ds(0, mats), pl.ds(0, 7 * HALF), :], ring_s.at[self.number])
            sent(wb.at[pl.ds(0, 1), pl.ds(0, 16 * HALF), :], x_s.at[self.number])
            sent(wb.at[pl.ds(0, 2), pl.ds(0, 8 * DEPTH), :], sib_s.at[self.number])
            if self.quarter:
                sent(wb.at[pl.ds(0, 1), pl.ds(0, 8 * HALF), :], xx_s)

    def out_move(block):
        rows = pl.ds(pl.multiple_of(half * HALF, 16), HALF)
        there = pl.ds(pl.multiple_of(block * DEPTH + half * HALF, 16), HALF)
        return lw_ref.at[pl.ds(3, 1), rows, :], wb.at[pl.ds(3, 1), there, :]

    def out_local():
        return pltpu.make_async_copy(*out_move(r), perm_r.at[11])

    def out_remote():
        return remote(*out_move(y_lo * 8 + core * 4 + z_lo), perm_s.at[11], perm_r.at[11], out_to)

    def out_start():
        @pl.when(out_stays)
        def _():
            out_local().start()

        @pl.when(out_moves)
        def _():
            out_remote().start()

    def out_wait():
        @pl.when(out_stays)
        def _():
            out_local().wait()

        @pl.when(out_moves)
        def _():
            arrived(out_move(r)[1], perm_r.at[11])

    keyval = Chunk(0, lw_ref, 1, 2, False)
    query_out = Chunk(1, lw_ref, 0, 3, False)
    res_kv = Chunk(2, rw_ref, 1, 2, True)
    res_qo = Chunk(3, rw_ref, 0, 3, False)
    W_KEY, W_VALUE, W_QUERY, W_OUT, R_KEY, R_VALUE, R_QUERY, R_OUT = range(8)

    keyval.perm_start()
    query_out.perm_start()
    out_start()
    for load in loads:
        load.wait()
    cos_o, sin_o = co_ref[pl.ds(r, 1), :], so_ref[pl.ds(r, 1), :]
    cos_part = ci_ref[...] * cos_o - si_ref[...] * sin_o
    sin_part = si_ref[...] * cos_o + ci_ref[...] * sin_o
    lat_normed = normalised(lat_ref[...].astype(F32), gain_ref[2:3, :], bias_ref[2:3, :]).astype(BF16)
    lat_cols = pl.ds(pl.multiple_of(ten * SLICE, 128), SLICE)
    lat32[...] = lat_ref[:, lat_cols].astype(F32)
    keyval.perm_wait()
    keyval.step(0)
    res_kv.perm_start()
    res_qo.perm_start()

    @pl.when(native)
    def _():
        for k in range(3):
            x_copy(k).start()
            x_local(k).start()

    keyval.step(1)
    query_out.perm_wait()
    out_wait()
    query_out.step(0)
    keyval.step(2)
    query_out.step(1)

    @pl.when(native)
    def _():
        for k in range(3):
            x_local(k).wait()

    @pl.when(moved)
    def _():
        for k in range(3):
            x_copy(k).wait_recv()

    keyval.step(3)
    query_out.step(2)
    keyval.step(4)
    query_out.step(3)
    normed = normalised(xb[...].astype(F32), gain_ref[0:1, :], bias_ref[0:1, :]).astype(BF16)
    keyval.finish()
    res_kv.perm_wait()
    res_kv.step(0)

    lane = lax.broadcasted_iota(jnp.int32, (ROWS, COLS), 1)
    low = lax.rem(lane, HDIM) < HDIM // 2

    def turn(a):
        swapped = jnp.where(
            low, -pltpu.roll(a, COLS - HDIM // 2, 1), pltpu.roll(a, HDIM // 2, 1)
        )
        return a * cos_part + swapped * sin_part

    def project(rows, matrix):
        return jnp.dot(rows, wb[matrix], preferred_element_type=F32)

    K_PART, V_PART = pl.ds(0, ROWS + 16), pl.ds(ROWS + 16, ROWS)

    def kv_start(index, part):
        rows = (K_PART, V_PART)[part]
        if index == 0:
            hops = [(1, 1), (2, 2)]
        elif index <= 4:
            hops = [(index + 2, index + 2)]
        elif index == 5 and part == 0:
            hops = [(7, 7)]
        elif index == 6 and part == 1:
            hops = [(7, 8)]
        else:
            hops = []
        for arriving, way in hops:
            src, dst = kvb.at[2 * index, rows, :], kvb.at[2 * arriving, rows, :]
            target = right if way % 2 else left
            begin(remote(src, dst, kv_s, kv_r.at[part, arriving], target))

    def kv_wait(index, part):
        arrived(kvb.at[2 * index, (K_PART, V_PART)[part], :], kv_r.at[part, index])

    def kv_sib_start(index):
        begin(remote(kvb.at[2 * index], kvb.at[2 * index + 1], kvs_s, kvs_r.at[index], sibling))

    def kv_sib_wait(index):
        arrived(kvb.at[2 * index + 1], kvs_r.at[index])

    def kv_step(number):
        for part in range(2):
            for index in (2 * number - 1, 2 * number):
                if index <= 7:
                    kv_wait(index, part)
                    kv_start(index, part)
        for index in (2 * number - 1, 2 * number):
            if index <= 7:
                kv_sib_start(index)

    chains = chain_row[...].astype(F32)
    valid = valid_row[...] > 0
    key_tag = jnp.where(valid, chains, -1.0)
    kvb[0, 0:ROWS, :] = turn(project(normed, W_KEY)).astype(BF16)
    kvb[0, ROWS : ROWS + 16, :] = jnp.broadcast_to(jnp.concatenate([key_tag] * 3, axis=1), (16, COLS)).astype(BF16)
    kv_start(0, 0)
    kvb[0, ROWS + 16 :, :] = project(normed, W_VALUE).astype(BF16)
    kv_start(0, 1)
    kv_sib_start(0)
    query_out.step(4)
    res_kv.step(1)
    query_out.finish()
    queries = turn(project(normed, W_QUERY) * (HDIM ** -0.5)).astype(BF16)
    stacked = [pair_stack(queries[:, p * 128 : (p + 1) * 128]) for p in range(3)]

    row_at = lax.broadcasted_iota(jnp.int32, (ROWS, ROWS), 0)
    col_at = lax.broadcasted_iota(jnp.int32, (ROWS, ROWS), 1)
    eye = row_at == col_at
    own_chain = jnp.sum(jnp.where(eye, jnp.broadcast_to(chains, (ROWS, ROWS)), 0.0), axis=1, keepdims=True)
    state = [None] * 3

    def attend(first, last):
        count = last - first
        pieces = []
        for slot in range(first, last):
            tag = kvb[slot, ROWS : ROWS + 16, 0:ROWS].astype(F32)[0:1, :]
            allowed = own_chain == tag
            if slot == 0:
                allowed = allowed | eye
            pieces.append(jnp.where(allowed, 0.0, NEGATIVE))
        bias = jnp.concatenate(pieces, axis=1)
        bias = jnp.concatenate([bias, bias], axis=0)
        for pair in range(3):
            cols = slice(pair * 128, (pair + 1) * 128)
            keys = kvb[first:last, 0:ROWS, cols].reshape(count * ROWS, 128)
            values = kvb[first:last, ROWS + 16 :, cols].reshape(count * ROWS, 128)
            scores = contract_last(stacked[pair], keys) + bias
            top = jnp.max(scores, axis=1, keepdims=True)
            if state[pair] is not None:
                top = jnp.maximum(top, state[pair][0])
            unrounded = jnp.exp(scores - top)
            totals = jnp.sum(unrounded, axis=1, keepdims=True)
            mixed = jnp.dot(unrounded.astype(BF16), values, preferred_element_type=F32)
            if state[pair] is not None:
                before, former, numerator = state[pair]
                scale = jnp.exp(before - top)
                totals = totals + former * scale
                mixed = mixed + numerator * scale
            state[pair] = top, totals, mixed

    kv_step(1)
    res_kv.step(2)
    kv_sib_wait(0)
    attend(0, 2)
    kv_step(2)
    res_kv.step(3)
    for index in (1, 2):
        kv_sib_wait(index)
    attend(2, 6)
    kv_step(3)
    res_kv.step(4)
    res_qo.perm_wait()
    res_qo.step(0)
    for index in (3, 4):
        kv_sib_wait(index)
    attend(6, 10)
    kv_step(4)
    for index in (5, 6):
        kv_sib_wait(index)
    attend(10, 14)
    res_qo.step(1)
    kv_sib_wait(7)
    attend(14, 16)
    pair_lane = lax.broadcasted_iota(jnp.int32, (ROWS, ROWS), 1)
    for pair in range(3):
        top, totals, mixed = state[pair]
        mixed = mixed / totals
        cols = slice(pair * 128, (pair + 1) * 128)
        att[group, :, cols] = jnp.where(pair_lane < HDIM, mixed[0:ROWS], mixed[ROWS:]).astype(BF16)

    parts = [pl.ds(0, ROWS // 2), pl.ds(ROWS // 2, ROWS // 2)]
    for h, rows in enumerate(parts):
        for offset in range(1, 4):
            ref = att.at[group, rows, :]
            begin(remote(ref, ref, rs_s, rs_r.at[h, offset], group_device(peer(offset))))
    res_kv.finish()
    res_qo.step(2)
    own_cols = pl.ds(pl.multiple_of(group * SLICE, 128), SLICE)

    def head_terms(g, rows):
        out_rows = pl.ds(pl.multiple_of(g * SLICE, 128), SLICE)
        return contract_last(att[g, rows, :], wb[W_OUT, out_rows, :])

    for h, rows in enumerate(parts):
        updated = xb[rows, own_cols].astype(F32) + head_terms(group, rows)
        for offset in range(1, 4):
            source = peer(4 - offset)
            arrived(att.at[source, rows, :], rs_r.at[h, offset])
            updated = updated + head_terms(source, rows)
        hb[group, rows, :] = updated.astype(BF16)
        for offset in range(1, 4):
            ref = hb.at[group, rows, :]
            begin(remote(ref, ref, ag_s, ag_r.at[h, offset], group_device(peer(offset))))
    res_qo.step(3)
    res_qo.step(4)
    for h, rows in enumerate(parts):
        for offset in range(1, 4):
            arrived(hb.at[peer(4 - offset), rows, :], ag_r.at[h, offset])
        whole = [hb[part, rows, :].astype(F32) for part in range(4)]
        average = sum(jnp.sum(w, axis=1, keepdims=True) for w in whole) / WIDTH
        centred = [w - average for w in whole]
        variance = sum(jnp.sum(c * c, axis=1, keepdims=True) for c in centred) / WIDTH
        scale = lax.rsqrt(variance + EPSILON)
        for part in range(4):
            cols = slice(part * SLICE, (part + 1) * SLICE)
            rn[rows, cols] = (centred[part] * scale * gain_ref[1:2, cols] + bias_ref[1:2, cols]).astype(BF16)

    def to_sibling():
        return remote(hb.at[y_lo * 2 + 1 - core], ho, ho_s, ho_r, sibling)

    def hidden_out(src):
        return pltpu.make_async_copy(src, hid_ref, load_s.at[1])

    @pl.when(native)
    def _():
        to_sibling().start()
        hidden_out(hb.at[group]).start()

    residue_normed = rn[...]
    rkv[0] = project(residue_normed, R_KEY).astype(BF16)
    rkv[1] = project(residue_normed, R_VALUE).astype(BF16)
    res_qo.finish()
    lq[...] = (project(lat_normed, R_QUERY) * (HDIM ** -0.5)).astype(BF16)

    usable = jnp.broadcast_to(valid, (2 * ROWS, ROWS))
    packed = jnp.zeros((ROWS, 128), F32)
    parts = []
    for pair in range(3):
        cols = slice(pair * 128, (pair + 1) * 128)
        scores = contract_last(pair_stack(lq[:, cols]), rkv[0, :, cols])
        scores = jnp.where(usable, scores, NEGATIVE)
        top = jnp.max(scores, axis=1, keepdims=True).astype(BF16).astype(F32)
        unrounded = jnp.where(usable, jnp.exp(scores - top), 0.0)
        totals = jnp.sum(unrounded, axis=1, keepdims=True)
        high = totals.astype(BF16).astype(F32)
        mixed = jnp.dot(unrounded.astype(BF16), rkv[1, :, cols], preferred_element_type=F32)
        parts.append(jnp.where(pair_lane < HDIM, mixed[0:ROWS], mixed[ROWS:]))
        for which in range(2):
            part = slice(which * ROWS, (which + 1) * ROWS)
            head = 2 * pair + which
            packed = jnp.where(pair_lane == head, top[part], packed)
            packed = jnp.where(pair_lane == 16 + head, high[part], packed)
            packed = jnp.where(pair_lane == 32 + head, (totals - high)[part], packed)
    parts.append(packed)
    pk[...] = jnp.concatenate([p.reshape(BLOCKS, 8, 128) for p in parts], axis=1).astype(BF16)

    @pl.when(moved)
    def _():
        arrived(ho, ho_r)
        hidden_out(ho).start()

    def block_rows(block):
        return pl.ds(pl.multiple_of(block * 8, 8), 8)

    for offset in range(1, 16):
        to = lax.rem(r + offset, 16)
        device = dev(y_hi, y_lo, lax.rem(to, 8), lax.div(to, 8))
        begin(remote(pk.at[to], rb.at[r], a2_s, a2_r, device))
    rb[r] = pk[r]
    arrived(rb.at[0:15], a2_r)

    received = rb[...].astype(F32)
    stats = received[:, 24:32, :]
    small_lane = lax.broadcasted_iota(jnp.int32, (BLOCKS, 8, 128), 2)
    pieces = []
    for pair in range(3):
        def spread(first_lane):
            return jnp.where(
                small_lane < HDIM,
                stats[:, :, first_lane : first_lane + 1],
                stats[:, :, first_lane + 1 : first_lane + 2],
            )

        tops = spread(2 * pair)
        weight = jnp.exp(tops - jnp.max(tops, axis=0, keepdims=True))
        total = jnp.sum((spread(16 + 2 * pair) + spread(32 + 2 * pair)) * weight, axis=0)
        mixed = jnp.sum(received[:, 8 * pair : 8 * pair + 8, :] * weight, axis=0)
        pieces.append(mixed / total)
    merged = jnp.concatenate(pieces, axis=1)
    merged = jnp.concatenate([merged, merged], axis=0).astype(BF16)
    for part in range(4):
        lp[part] = contract_last(merged, wb[R_OUT, part * SLICE : (part + 1) * SLICE, :])[0:8]

    def out_copy(part):
        owner = (x, r, jnp.int32(part))
        return remote(lp.at[part], lb.at[group], lo_s.at[part], lo_r.at[group], owner)

    for part in range(4):
        mine = native & (ten == part)

        @pl.when(mine)
        def _():
            lb[group] = lp[part]

        @pl.when(jnp.logical_not(mine))
        def _():
            out_copy(part).start()

    for chunk in (keyval, query_out, res_kv, res_qo):
        chunk.all_sent()
    sent(kvb.at[0:7], kv_s)
    sent(kvb.at[0:8], kvs_s)
    sent(att.at[0:3], rs_s)
    sent(hb.at[0:3], ag_s)
    sent(rb.at[0:15], a2_s)

    @pl.when(native)
    def _():
        for k in range(3):
            x_copy(k).wait_send()
        to_sibling().wait_send()
        hidden_out(hb.at[group]).wait()

    @pl.when(moved)
    def _():
        for chunk in (keyval, query_out, res_kv, res_qo):
            for copy in chunk.perm_copies():
                copy.wait_send()
        hidden_out(ho).wait()

    @pl.when(out_moves)
    def _():
        out_remote().wait_send()

    for part in range(4):
        mine = native & (group == part)

        @pl.when(jnp.logical_not(mine))
        def _():
            arrived(lb.at[part], lo_r.at[part])

    total = lat32[block_rows(ctx), :]
    for part in range(4):
        total = total + lb[part]
    fin[...] = total.astype(BF16)
    last = pltpu.make_async_copy(fin, out_ref, load_s.at[0])
    last.start()
    for part in range(4):
        mine = native & (ten == part)

        @pl.when(jnp.logical_not(mine))
        def _():
            out_copy(part).wait_send()
    last.wait()


def per_device(
    residues, chain_ids, residue_valid, layer_weights, resampler_weights, norm_gains, norm_biases, latents
):
    tables = [jnp.asarray(t) for t in angle_tables()]
    hbm = pl.BlockSpec(memory_space=pl.ANY)
    dma = pltpu.SemaphoreType.DMA
    return pl.pallas_call(
        kernel,
        out_shape=(
            jax.ShapeDtypeStruct((ROWS, SLICE), BF16),
            jax.ShapeDtypeStruct((8, SLICE), BF16),
        ),
        in_specs=[hbm] * 12,
        out_specs=(hbm, hbm),
        scratch_shapes=[
            pltpu.VMEM((8, WIDTH, COLS), BF16),
            pltpu.VMEM((ROWS, WIDTH), BF16),
            pltpu.VMEM((1, ROWS), jnp.int32),
            pltpu.VMEM((1, ROWS), jnp.int32),
            pltpu.VMEM((3, WIDTH), F32),
            pltpu.VMEM((3, WIDTH), F32),
            pltpu.VMEM((ROWS, WIDTH), BF16),
            pltpu.VMEM((ROWS, COLS), F32),
            pltpu.VMEM((ROWS, COLS), F32),
            pltpu.VMEM((BLOCKS, COLS), F32),
            pltpu.VMEM((BLOCKS, COLS), F32),
            pltpu.VMEM((BLOCKS, 2 * ROWS + 16, COLS), BF16),
            pltpu.VMEM((4, ROWS, COLS), BF16),
            pltpu.VMEM((4, ROWS, SLICE), BF16),
            pltpu.VMEM((ROWS, SLICE), BF16),
            pltpu.VMEM((ROWS, WIDTH), BF16),
            pltpu.VMEM((ROWS, COLS), BF16),
            pltpu.VMEM((2, ROWS, COLS), BF16),
            pltpu.VMEM((BLOCKS, 32, 128), BF16),
            pltpu.VMEM((BLOCKS, 32, 128), BF16),
            pltpu.VMEM((4, 8, SLICE), F32),
            pltpu.VMEM((4, 8, SLICE), F32),
            pltpu.VMEM((ROWS, SLICE), F32),
            pltpu.VMEM((8, SLICE), BF16),
            dma((7,)),
            dma((12,)), dma((12,)),
            dma((4,)), dma((4, 8)),
            dma((4,)), dma((4, 8)),
            dma, dma((8,)),
            dma((4,)), dma((4,)),
            dma, dma((2, 8)),
            dma, dma((8,)),
            dma, dma((2, 4)),
            dma, dma((2, 4)),
            dma, dma,
            dma, dma,
            dma((4,)), dma((4,)),
        ],
        compiler_params=pltpu.CompilerParams(
            collective_id=0, has_side_effects=True, vmem_limit_bytes=56 * 1024 * 1024
        ),
    )(
        residues, chain_ids[None, :], residue_valid[None, :], layer_weights, resampler_weights,
        norm_gains, norm_biases, latents, *tables
    )


def solution(mesh):
    placed = (
        P(("dp", "ctx"), None),
        P(("dp", "ctx")),
        P(("dp", "ctx")),
        P(None, "ctx", "tensor"),
        P(None, "ctx", "tensor"),
        P(),
        P(),
        P(),
    )
    return jax.shard_map(
        per_device,
        mesh=mesh,
        in_specs=placed,
        out_specs=(P(("dp", "ctx"), "tensor"), P(("dp", "ctx"), "tensor")),
        check_vma=False,
    )
```
